32 devices in a mesh: member: 2 (over x), space: 16 (over z, y, core).
Axes of the slice: x: 2, y: 2, z: 4, core: 2. Of those that a mesh axis runs over, the one named last changes fastest.
Arguments:
- params: float32 [256, 64, 1024], P('member', 'space'), may hold values from -2 to 2
- state: float32 [256, 64, 1024], P('member', 'space'), may hold values from -6 to 6
- regime: int32 [64, 1024], P('space'), may hold values from 0 to 7
- regime_coefs: float32 [8, 4], replicated, may hold values from 0.1 to 0.5
- observation_index: int32 [8192], P('space'), may hold values from 0 to 65535, as said below
- measured_values: float32 [8192], P('space'), may hold values from -6 to 6
- observation_spread: float32 [8192], P('space'), may hold values from 0.1 to 1
- observation_jitter: float32 [256, 8192], P('member', 'space'), may hold values from -6 to 6
Outputs:
- revised_log_diffusivity: float32 [256, 64, 1024], P('member', 'space')
- predicted_member_state: float32 [256, 64, 1024], P('member', 'space')
The draws below stay inside these ranges and needn't reach their ends.
Inputs may be any that keep to these rules, and one draw needn't show every extreme that they name: `observation_index`: observation o lies in the strip of rows o // 512 * 4 up to (o // 512 + 1) * 4 - 1; the first observation of each strip sits on its first cell, the second on its last cell; cells may repeat.
All inputs are finite; a program needn't handle non-finite values.
Results may differ from the reference program's by a relative error of at most 0.015.
Values sent between devices are 32-bit elements; how exact they have to be, the bound alone decides.
A program may use at most 64 MiB of HBM per device.

```python
import math
import jax
import jax.numpy as jnp
from jax import lax

ROWS_DEV = 4
NCOLS = 1024
OBS_DEV = 512
REGIMES = 8
MEMBERS = 256
NROWS = 64
NOBS = 8192


def draw_observation_index(key, part):
    strip_cells = ROWS_DEV * NCOLS
    order = jnp.arange(NOBS, dtype=jnp.int32)
    strip = order // OBS_DEV
    position = order % OBS_DEV
    local_cell = jax.random.randint(key, (NOBS,), 0, strip_cells, dtype=jnp.int32)
    local_cell = jnp.where(position == 0, 0, jnp.where(position == 1, strip_cells - 1, local_cell))
    return (strip * strip_cells + local_cell).astype(jnp.int32)


def place_ends(drawn, stream_key, low, top_value):
    extent = drawn.shape
    spot = [jax.random.randint(jax.random.fold_in(stream_key, axis), (), 0, extent[axis]) for axis in range(len(extent))]
    drawn = drawn.at[tuple(spot)].set(low)
    longest = extent.index(max(extent))
    spot[longest] = (spot[longest] + 1) % extent[longest]
    return drawn.at[tuple(spot)].set(top_value)


def shard_levels(key, dims, split, low, top_value):
    gain, own = 1.0, jax.random.fold_in(key, 6)
    for dim, shards_of in split:
        steps = jnp.exp(jax.random.uniform(jax.random.fold_in(own, dim), (shards_of,), jnp.float32, low / len(split), top_value / len(split)))
        gain = gain * jnp.repeat(steps, dims[dim] // shards_of).reshape([-1 if axis == dim else 1 for axis in range(len(dims))])
    return gain


def scatter_about(rng, dims, width, reach, split=(), held_as=jnp.bfloat16):
    result = jax.random.normal(rng, dims, jnp.float32) * width
    if len(split) > 0:
        result = shard_levels(rng, dims, split, -0.22, 0.18) * result
    return jnp.clip(result, min=-reach, max=reach).astype(held_as)


def setup_inputs(seed: int = 0) -> dict:
    splits = jax.random.split(jax.random.key(seed), 9)
    params = scatter_about(splits[0], (MEMBERS, NROWS, NCOLS), 0.5, 2.0, ((0, 2), (1, 16)), jnp.float32)
    state = scatter_about(splits[1], (MEMBERS, NROWS, NCOLS), 1.0, 6.0, ((0, 2), (1, 16)), jnp.float32)
    regime = place_ends(jax.random.randint(splits[2], (NROWS, NCOLS), 0, REGIMES), jax.random.fold_in(splits[2], 1), 0, REGIMES - 1).astype(jnp.int32)
    regime_coefs = jnp.clip(jax.random.uniform(splits[3], (REGIMES, 4), jnp.float32, 0.1, 0.5), 0.1, 0.5)
    observation_index = draw_observation_index(jax.random.fold_in(splits[8], 71), 0)
    measured_values = scatter_about(splits[5], (NOBS,), 1.0, 6.0, ((0, 16),), jnp.float32)
    observation_spread = jnp.clip(jnp.exp(math.log(1.0) - 2.3025851 * jax.random.uniform(splits[6], (NOBS,), jnp.float32) ** shard_levels(splits[6], (NOBS,), ((0, 16),), -0.2, 0.2)), 0.1, 1.0)
    observation_jitter = scatter_about(splits[7], (MEMBERS, NOBS), 1.0, 6.0, ((0, 2), (1, 16)), jnp.float32)
    return {"params": params, "state": state, "regime": regime, "regime_coefs": regime_coefs, "observation_index": observation_index, "measured_values": measured_values, "observation_spread": observation_spread, "observation_jitter": observation_jitter}


time_step = 0.06

def coef_fields(regime, regime_coefs):
    levels = jnp.arange(regime_coefs.shape[0], dtype=jnp.int32)
    onehot = (regime[None, :, :] == levels[:, None, None]).astype(jnp.float32)
    return jnp.einsum('rd,rxy->dxy', regime_coefs, onehot, precision=lax.Precision.HIGHEST)

def advance(extended, rates, coefs):
    center = extended[..., 1:-1, :]
    widths = [(0, 0)] * (center.ndim - 1) + [(1, 1)]
    padded_cols = jnp.pad(center, widths)
    above = extended[..., :-2, :]
    below = extended[..., 2:, :]
    left_side = padded_cols[..., :-2]
    right_side = padded_cols[..., 2:]
    flow = coefs[0] * (above - center) + coefs[1] * (below - center)
    flow = flow + coefs[2] * (left_side - center) + coefs[3] * (right_side - center)
    return center + rates * flow

def reference(params, state, regime, regime_coefs, observation_index, measured_values, observation_spread, observation_jitter):
    coefs = coef_fields(regime, regime_coefs)

    def single_member(pair):
        member_params, member_state = pair
        rates = time_step * jnp.exp(member_params)
        current = member_state
        for repeat in range(2):
            current = advance(jnp.pad(current, ((1, 1), (0, 0))), rates, coefs)
        return current
    predicted_member_state = lax.map(single_member, (params, state))
    member_list = params.shape[0]
    square_root_scale = math.sqrt(member_list - 1)
    flattened_grid = predicted_member_state.reshape(member_list, -1)
    predicted_fields = jnp.take(flattened_grid, observation_index, axis=1)
    ensemble_mean_prediction = lax.optimization_barrier(jnp.sum(predicted_fields, axis=0)) / member_list
    member_departures = (predicted_fields - ensemble_mean_prediction[None, :]) / (observation_spread[None, :] * square_root_scale)
    observation_misfits = (measured_values[None, :] + observation_spread[None, :] * observation_jitter - predicted_fields) / observation_spread[None, :]
    stacked = jnp.concatenate([member_departures, observation_misfits], axis=0)
    gram_full = jnp.dot(member_departures.astype(jnp.float32), stacked.T.astype(jnp.float32), precision=lax.Precision.HIGHEST, preferred_element_type=jnp.float32)
    gram = gram_full[:, :member_list]
    cross = gram_full[:, member_list:]
    system = jnp.eye(member_list, dtype=jnp.float32) + gram
    factor = jnp.linalg.cholesky(system)
    mixing = jax.scipy.linalg.cho_solve((factor, True), cross)
    param_anom = params / square_root_scale
    update = jnp.einsum('kj,kxy->jxy', mixing, param_anom, precision=lax.Precision.HIGHEST)
    revised_log_diffusivity = params + update
    return (revised_log_diffusivity, predicted_member_state)
```

```python
import math

import jax
import jax.numpy as jnp
from jax import lax
from jax.sharding import PartitionSpec as P

time_step = 0.06


def with_halo(cells, sides, width):
    for axis, dim in sides:
        count = lax.axis_size(axis)
        ends = count - 1
        head = lax.slice_in_dim(cells, 0, width, axis=dim)
        tail = lax.slice_in_dim(cells, cells.shape[dim] - width, cells.shape[dim], axis=dim)
        cells = jnp.concatenate(
            [
                lax.ppermute(tail, axis, [(i, (i + 1) % count) for i in range(ends)]),
                cells,
                lax.ppermute(head, axis, [((i + 1) % count, i) for i in range(ends)]),
            ],
            axis=dim,
        )
    return cells


def coef_fields(regime, regime_coefs):
    levels = jnp.arange(regime_coefs.shape[0], dtype=jnp.int32)
    onehot = (regime[None, :, :] == levels[:, None, None]).astype(jnp.float32)
    return jnp.einsum("rd,rxy->dxy", regime_coefs, onehot, precision=lax.Precision.HIGHEST)


def advance(extended, rates, coefs):
    center = extended[..., 1:-1, :]
    widths = [(0, 0)] * (center.ndim - 1) + [(1, 1)]
    padded_cols = jnp.pad(center, widths)
    above = extended[..., :-2, :]
    below = extended[..., 2:, :]
    left_side = padded_cols[..., :-2]
    right_side = padded_cols[..., 2:]
    flow = coefs[0] * (above - center) + coefs[1] * (below - center)
    flow = flow + coefs[2] * (left_side - center) + coefs[3] * (right_side - center)
    return center + rates * flow


def body(
    params,
    state,
    regime,
    regime_coefs,
    observation_index,
    measured_values,
    observation_spread,
    observation_jitter,
):
    block_members = params.shape[0]
    strip_rows = params.shape[1]
    columns = params.shape[2]
    member_list = block_members * lax.axis_size("member")
    square_root_scale = math.sqrt(member_list - 1)
    coefs = coef_fields(regime, regime_coefs)
    rates = time_step * jnp.exp(params)
    current = state
    for repeat in range(2):
        extended = with_halo(current, (("space", 1),), 1)
        current = advance(extended, rates, coefs)
    slab_local_index = observation_index - lax.axis_index("space") * (strip_rows * columns)
    flattened_grid = current.reshape(block_members, strip_rows * columns)
    own = jnp.take(flattened_grid, slab_local_index, axis=1)
    swap = [(0, 1), (1, 0)]
    theirs = lax.ppermute(own, "member", swap)
    total = jnp.sum(own, axis=0) + jnp.sum(theirs, axis=0)
    mean = total / member_list
    fields = jnp.concatenate([own, theirs], axis=0)
    departures = (fields - mean[None, :]) / (observation_spread[None, :] * square_root_scale)
    misfits = (
        measured_values[None, :] + observation_spread[None, :] * observation_jitter - own
    ) / observation_spread[None, :]
    stacked = jnp.concatenate([departures, misfits], axis=0)
    rows = jnp.dot(
        departures, stacked.T, precision=lax.Precision.HIGHEST, preferred_element_type=jnp.float32
    )
    rows = lax.psum(rows, "space")
    params_theirs = lax.ppermute(params, "member", swap)
    system = jnp.eye(member_list, dtype=jnp.float32) + rows[:, :member_list]
    factor = jnp.linalg.cholesky(system)
    mixing = jax.scipy.linalg.cho_solve((factor, True), rows[:, member_list:])
    piece = jnp.concatenate([params, params_theirs], axis=0) / square_root_scale
    update = jnp.einsum("kj,kxy->jxy", mixing, piece, precision=lax.Precision.HIGHEST)
    return (params + update, current)


def solution(mesh):
    in_specs = (
        P("member", "space", None),
        P("member", "space", None),
        P("space", None),
        P(),
        P("space"),
        P("space"),
        P("space"),
        P("member", "space"),
    )
    out_specs = (P("member", "space", None), P("member", "space", None))
    return jax.shard_map(body, mesh=mesh, in_specs=in_specs, out_specs=out_specs, check_vma=False)
```

```python
import functools
import math

import jax
import jax.numpy as jnp
from jax import lax
from jax.experimental import pallas as pl
from jax.experimental.pallas import tpu as pltpu
from jax.sharding import PartitionSpec as P

time_step = 0.06
MESH = pl.DeviceIdType.MESH
HIGHEST = lax.Precision.HIGHEST
HALO_PARTS = 4
PARAM_PARTS = 16
GROUP = 16


def forward_kernel(
    n, low, high, params, state, regime, regime_coefs, index, measured, spread, jitter,
    state_out, params_theirs_out, sums_out,
    mid, rates, coef, from_up, from_down, params_theirs, onehot, split, picked, own, theirs,
    stacked, part, landed, landed_high, total,
    halo_send, halo_recv, params_send, params_recv, field_send, field_recv, sum_send, sum_recv,
):
    members, cells = state.shape
    rows = regime.shape[0]
    columns = cells // rows
    me = lax.axis_index("space")
    up = lax.rem(me + n - 1, n)
    down = lax.rem(me + 1, n)
    twin = {"member": 1 - lax.axis_index("member")}
    bits = [lax.rem(lax.div(me, 1 << t), 2) for t in range(low + high)]
    pairs = [me + (1 - 2 * bits[t]) * (1 << t) for t in range(low + high)]

    barrier = pltpu.get_barrier_semaphore()
    greeted = [twin, {"space": up}, {"space": down}] + [{"space": q} for q in pairs]
    for device in greeted:
        pl.semaphore_signal(barrier, inc=1, device_id=device, device_id_type=MESH)
    pl.semaphore_wait(barrier, len(greeted))

    def send(src, dst, ssem, rsem, device):
        copy = pltpu.make_async_remote_copy(
            src_ref=src, dst_ref=dst, send_sem=ssem, recv_sem=rsem,
            device_id=device, device_id_type=MESH,
        )
        copy.start()
        return copy

    block = members // HALO_PARTS

    def halo(src, phase, c):
        span = pl.ds(c * block, block)
        return [
            send(src.at[span, pl.ds(cells - columns, columns)], from_up.at[phase, span],
                 halo_send.at[phase, 0, c], halo_recv.at[phase, 0, c], {"space": down}),
            send(src.at[span, pl.ds(0, columns)], from_down.at[phase, span],
                 halo_send.at[phase, 1, c], halo_recv.at[phase, 1, c], {"space": up}),
        ]

    params_rows = members // PARAM_PARTS
    params_copies = []

    def send_params(stop):
        for c in range(len(params_copies), stop):
            span = pl.ds(c * params_rows, params_rows)
            params_copies.append(send(params.at[span], params_theirs.at[span],
                                      params_send.at[c], params_recv.at[c], twin))

    first = [halo(state, 0, c) for c in range(HALO_PARTS)]
    send_params(6)

    for d in range(4):
        value = jnp.zeros(regime.shape, jnp.float32)
        for k in range(regime_coefs.shape[0]):
            value = jnp.where(regime[...] == k, regime_coefs[k, d], value)
        coef[d] = value

    observations = index.shape[1]
    local = index[...] - me * cells
    height = 256

    @pl.loop(0, cells // height)
    def _(b):
        start = pl.multiple_of(b * height, height)
        cell = lax.broadcasted_iota(jnp.int32, (height, observations), 0) + start
        onehot[pl.ds(start, height), :] = jnp.where(cell == local, 1.0, 0.0).astype(jnp.bfloat16)

    column = lax.broadcasted_iota(jnp.int32, (GROUP, columns), 1)

    def advance(src, phase, c):
        @pl.loop(0, block // GROUP)
        def _(g):
            start = pl.multiple_of(c * block + g * GROUP, GROUP)
            span = pl.ds(start, GROUP)
            for r in range(rows):
                here = pl.ds(r * columns, columns)
                x = src[span, here]
                if r > 0:
                    above = src[span, pl.ds((r - 1) * columns, columns)]
                else:
                    above = jnp.where(me > 0, from_up[phase, span, :], 0.0)
                if r < rows - 1:
                    below = src[span, pl.ds((r + 1) * columns, columns)]
                else:
                    below = jnp.where(me < n - 1, from_down[phase, span, :], 0.0)
                left = jnp.where(column == 0, 0.0, pltpu.roll(x, 1, 1))
                right = jnp.where(column == columns - 1, 0.0, pltpu.roll(x, columns - 1, 1))
                row = pl.ds(r, 1)
                flow = coef[0, row, :] * (above - x) + coef[1, row, :] * (below - x)
                flow = flow + coef[2, row, :] * (left - x) + coef[3, row, :] * (right - x)
                if phase == 0:
                    rate = time_step * jnp.exp(params[span, here])
                    rates[span, here] = rate
                    mid[span, here] = x + rate * flow
                else:
                    value = x + rates[span, here] * flow
                    state_out[span, here] = value
                    top = value.astype(jnp.bfloat16)
                    rest = value - top.astype(jnp.float32)
                    middle = rest.astype(jnp.bfloat16)
                    last = (rest - middle.astype(jnp.float32)).astype(jnp.bfloat16)
                    split[span, here] = top
                    split[pl.ds(start + members, GROUP), here] = middle
                    split[pl.ds(start + 2 * members, GROUP), here] = last

    second = []
    for c in range(HALO_PARTS):
        for copy in first[c]:
            copy.wait()
        advance(state, 0, c)
        second.append(halo(mid, 1, c))
        if c == 1:
            send_params(9)
    for c in range(HALO_PARTS):
        for copy in second[c]:
            copy.wait()
        advance(mid, 1, c)

    picked[...] = jnp.zeros_like(picked)
    depth = 1024

    @pl.loop(0, cells // depth)
    def _(b):
        span = pl.ds(pl.multiple_of(b * depth, depth), depth)
        picked[...] += jnp.dot(split[:, span], onehot[span, :], preferred_element_type=jnp.float32)

    own[...] = (picked[:members] + picked[members : 2 * members]) + picked[2 * members :]
    field = send(own, theirs, field_send, field_recv, twin)
    send_params(PARAM_PARTS)
    field.wait()

    everyone = 2 * members
    root = math.sqrt(everyone - 1)
    mean = (jnp.sum(own[...], axis=0, keepdims=True) + jnp.sum(theirs[...], axis=0, keepdims=True)) / everyone
    inverse = 1.0 / spread[...]
    scale = inverse / root
    stacked[:members] = (own[...] - mean) * scale
    stacked[members:everyone] = (theirs[...] - mean) * scale
    stacked[everyone:] = (measured[...] - own[...]) * inverse + jitter[...]
    contract = (((1,), (1,)), ((), ()))
    for h in range(2):
        part[h * members : (h + 1) * members] = lax.dot_general(
            stacked[h * members : (h + 1) * members], stacked[...], contract,
            precision=HIGHEST, preferred_element_type=jnp.float32,
        )

    start = 0
    size = everyone
    used = 0
    for t in range(low):
        size //= 2
        keep = pl.multiple_of(start + bits[t] * size, size)
        give = pl.multiple_of(start + (1 - bits[t]) * size, size)
        copy = send(part.at[pl.ds(give, size)], landed.at[pl.ds(used, size)],
                    sum_send.at[t], sum_recv.at[t], {"space": pairs[t]})
        copy.wait()
        part[pl.ds(keep, size)] = part[pl.ds(keep, size)] + landed[pl.ds(used, size)]
        used += size
        start = keep
    mine = pl.ds(start, size)
    for t in range(low, low + high):
        copy = send(part.at[mine], landed_high.at[t - low],
                    sum_send.at[t], sum_recv.at[t], {"space": pairs[t]})
        copy.wait()
        part[mine] = part[mine] + landed_high[t - low]
    total[mine] = part[mine]
    for t in reversed(range(low)):
        span = pl.ds(pl.multiple_of(start, size), size)
        slot = low + high + t
        copy = send(total.at[span], total.at[span],
                    sum_send.at[slot], sum_recv.at[slot], {"space": pairs[t]})
        copy.wait()
        start = start - bits[t] * size
        size *= 2
    sums_out[...] = total[...]
    for copy in params_copies:
        copy.wait()
    params_theirs_out[...] = params_theirs[...]


def solve_kernel(sums, params, params_theirs, out, work):
    everyone = sums.shape[0]
    members = everyone // 2
    width = sums.shape[1]
    r = lax.broadcasted_iota(jnp.int32, (everyone, width), 0)
    c = lax.broadcasted_iota(jnp.int32, (everyone, width), 1)
    work[...] = sums[...] + jnp.where(r == c, 1.0, 0.0)
    size = 32
    row = lax.broadcasted_iota(jnp.int32, (size, 2 * size), 0)
    lane = lax.broadcasted_iota(jnp.int32, (size, 2 * size), 1)
    unit = lax.broadcasted_iota(jnp.int32, (size, size), 0) == lax.broadcasted_iota(jnp.int32, (size, size), 1)
    for b in range(everyone // size):
        at = b * size
        pivot = work[at : at + size, at : at + size]
        aug = jnp.concatenate([pivot, jnp.where(unit, 1.0, 0.0)], axis=1)
        for k in range(size):
            line = aug[k : k + 1, :] / aug[k : k + 1, k : k + 1]
            aug = jnp.where(row == k, line, aug - aug[:, k : k + 1] * line)
        inverse = aug[:, size:]
        begin = (at + size) // 128 * 128
        lines = jnp.dot(inverse, work[at : at + size, begin:], precision=HIGHEST, preferred_element_type=jnp.float32)
        change = jnp.dot(work[:, at : at + size], lines, precision=HIGHEST, preferred_element_type=jnp.float32)
        work[:, begin:] = work[:, begin:] - change
        work[at : at + size, begin:] = lines
    mixing = work[:, everyone:] / math.sqrt(everyone - 1)
    weights = mixing.T
    tile = 512

    @pl.loop(0, params.shape[1] // tile)
    def _(b):
        span = pl.ds(pl.multiple_of(b * tile, tile), tile)
        out[:, span] = params[:, span] + (
            jnp.dot(weights[:, :members], params[:, span], precision=HIGHEST, preferred_element_type=jnp.float32)
            + jnp.dot(weights[:, members:], params_theirs[:, span], precision=HIGHEST, preferred_element_type=jnp.float32)
        )


def body(n, params, state, regime, regime_coefs, index, measured, spread, jitter):
    members, rows, columns = params.shape
    cells = rows * columns
    observations = index.shape[0]
    everyone = 2 * members
    levels = n.bit_length() - 1
    low = min(levels, 4)
    high = levels - low
    f32 = jnp.float32
    flat_params = params.reshape(members, cells)
    flat_state = state.reshape(members, cells)
    vmem = pl.BlockSpec(memory_space=pltpu.VMEM)
    smem = pl.BlockSpec(memory_space=pltpu.SMEM)
    width = everyone + members
    last = everyone >> low
    sems = pltpu.SemaphoreType.DMA
    flat_out, theirs, sums = pl.pallas_call(
        functools.partial(forward_kernel, n, low, high),
        out_shape=[
            jax.ShapeDtypeStruct((members, cells), f32),
            jax.ShapeDtypeStruct((members, cells), f32),
            jax.ShapeDtypeStruct((everyone, width), f32),
        ],
        in_specs=[vmem, vmem, vmem, smem, vmem, vmem, vmem, vmem],
        out_specs=[vmem, vmem, vmem],
        scratch_shapes=[
            pltpu.VMEM((members, cells), f32),
            pltpu.VMEM((members, cells), f32),
            pltpu.VMEM((4, rows, columns), f32),
            pltpu.VMEM((2, members, columns), f32),
            pltpu.VMEM((2, members, columns), f32),
            pltpu.VMEM((members, cells), f32),
            pltpu.VMEM((cells, observations), jnp.bfloat16),
            pltpu.VMEM((3 * members, cells), jnp.bfloat16),
            pltpu.VMEM((3 * members, observations), f32),
            pltpu.VMEM((members, observations), f32),
            pltpu.VMEM((members, observations), f32),
            pltpu.VMEM((3 * members, observations), f32),
            pltpu.VMEM((everyone, width), f32),
            pltpu.VMEM((everyone, width), f32),
            pltpu.VMEM((max(high, 1), last, width), f32),
            pltpu.VMEM((everyone, width), f32),
            sems((2, 2, HALO_PARTS)),
            sems((2, 2, HALO_PARTS)),
            sems((PARAM_PARTS,)),
            sems((PARAM_PARTS,)),
            sems,
            sems,
            sems((2 * low + high,)),
            sems((2 * low + high,)),
        ],
        compiler_params=pltpu.CompilerParams(
            collective_id=0, has_side_effects=True, vmem_limit_bytes=48 << 20
        ),
    )(flat_params, flat_state, regime, regime_coefs, index[None], measured[None], spread[None], jitter)
    revised = pl.pallas_call(
        solve_kernel,
        out_shape=jax.ShapeDtypeStruct((members, cells), f32),
        in_specs=[vmem, vmem, vmem],
        out_specs=vmem,
        scratch_shapes=[pltpu.VMEM((everyone, width), f32)],
        compiler_params=pltpu.CompilerParams(vmem_limit_bytes=32 << 20),
    )(sums, flat_params, theirs)
    return (revised.reshape(params.shape), flat_out.reshape(state.shape))


def solution(mesh):
    in_specs = (
        P("member", "space", None),
        P("member", "space", None),
        P("space", None),
        P(),
        P("space"),
        P("space"),
        P("space"),
        P("member", "space"),
    )
    out_specs = (P("member", "space", None), P("member", "space", None))
    return jax.shard_map(
        functools.partial(body, mesh.shape["space"]),
        mesh=mesh, in_specs=in_specs, out_specs=out_specs, check_vma=False,
    )
```

```python
import functools
import math

import jax
import jax.numpy as jnp
from jax import lax
from jax.experimental import pallas as pl
from jax.experimental.pallas import tpu as pltpu
from jax.sharding import PartitionSpec as P

time_step = 0.06
MESH = pl.DeviceIdType.MESH
HIGHEST = lax.Precision.HIGHEST
HALO_PARTS = 4
PARAM_PARTS = 16
GROUP = 16


def forward_kernel(
    n, low, high, params_hbm, state_hbm, regime, regime_coefs, index, measured, spread, jitter,
    state_out, theirs_out, sums_out,
    params, state, result, mid, rates, coef, from_up, from_down, onehot, split, picked, own, theirs,
    stacked, part, landed, landed_high, total,
    halo_send, halo_recv, params_send, params_recv, field_send, field_recv, sum_send, sum_recv, load_sem, store_sem,
):
    members, cells = params.shape
    rows = regime.shape[0]
    columns = cells // rows
    me = lax.axis_index("space")
    up = lax.rem(me + n - 1, n)
    down = lax.rem(me + 1, n)
    twin = {"member": 1 - lax.axis_index("member")}
    bits = [lax.rem(lax.div(me, 1 << t), 2) for t in range(low + high)]
    pairs = [me + (1 - 2 * bits[t]) * (1 << t) for t in range(low + high)]

    def rowwise(flat, whole, sem, outward):
        copies = []
        for r in range(rows):
            pair = (flat.at[:, pl.ds(r * columns, columns)], whole.at[:, r, :])
            src, dst = pair if outward else pair[::-1]
            copies.append(pltpu.make_async_copy(src, dst, sem.at[r]))
            copies[-1].start()
        return copies

    params_loads = rowwise(params, params_hbm, load_sem.at[0], False)
    state_loads = rowwise(state, state_hbm, load_sem.at[1], False)

    barrier = pltpu.get_barrier_semaphore()
    greeted = [twin, {"space": up}, {"space": down}] + [{"space": q} for q in pairs]
    for device in greeted:
        pl.semaphore_signal(barrier, inc=1, device_id=device, device_id_type=MESH)
    pl.semaphore_wait(barrier, len(greeted))

    def send(src, dst, ssem, rsem, device):
        copy = pltpu.make_async_remote_copy(
            src_ref=src, dst_ref=dst, send_sem=ssem, recv_sem=rsem,
            device_id=device, device_id_type=MESH,
        )
        copy.start()
        return copy

    block = members // HALO_PARTS

    def halo(src, phase, c):
        span = pl.ds(c * block, block)
        if phase == 0:
            bottom, top = src.at[span, rows - 1, :], src.at[span, 0, :]
        else:
            bottom, top = src.at[span, pl.ds(cells - columns, columns)], src.at[span, pl.ds(0, columns)]
        return [
            send(bottom, from_up.at[phase, span],
                 halo_send.at[phase, 0, c], halo_recv.at[phase, 0, c], {"space": down}),
            send(top, from_down.at[phase, span],
                 halo_send.at[phase, 1, c], halo_recv.at[phase, 1, c], {"space": up}),
        ]

    params_rows = members // PARAM_PARTS
    params_copies = []

    def send_params(stop):
        for c in range(len(params_copies), stop):
            span = pl.ds(c * params_rows, params_rows)
            params_copies.append(send(params_hbm.at[span], theirs_out.at[span],
                                      params_send.at[c], params_recv.at[c], twin))

    first = [halo(state_hbm, 0, c) for c in range(HALO_PARTS)]
    send_params(6)

    for d in range(4):
        value = jnp.zeros(regime.shape, jnp.float32)
        for k in range(regime_coefs.shape[0]):
            value = jnp.where(regime[...] == k, regime_coefs[k, d], value)
        coef[d] = value

    observations = index.shape[1]
    local = index[...] - me * cells
    height = 256

    @pl.loop(0, cells // height)
    def _(b):
        start = pl.multiple_of(b * height, height)
        cell = lax.broadcasted_iota(jnp.int32, (height, observations), 0) + start
        onehot[pl.ds(start, height), :] = jnp.where(cell == local, 1.0, 0.0).astype(jnp.bfloat16)

    column = lax.broadcasted_iota(jnp.int32, (GROUP, columns), 1)

    def advance(src, phase, c):
        @pl.loop(0, block // GROUP)
        def _(g):
            start = pl.multiple_of(c * block + g * GROUP, GROUP)
            span = pl.ds(start, GROUP)
            for r in range(rows):
                here = pl.ds(r * columns, columns)
                x = src[span, here]
                if r > 0:
                    above = src[span, pl.ds((r - 1) * columns, columns)]
                else:
                    above = jnp.where(me > 0, from_up[phase, span, :], 0.0)
                if r < rows - 1:
                    below = src[span, pl.ds((r + 1) * columns, columns)]
                else:
                    below = jnp.where(me < n - 1, from_down[phase, span, :], 0.0)
                left = jnp.where(column == 0, 0.0, pltpu.roll(x, 1, 1))
                right = jnp.where(column == columns - 1, 0.0, pltpu.roll(x, columns - 1, 1))
                row = pl.ds(r, 1)
                flow = coef[0, row, :] * (above - x) + coef[1, row, :] * (below - x)
                flow = flow + coef[2, row, :] * (left - x) + coef[3, row, :] * (right - x)
                if phase == 0:
                    rate = time_step * jnp.exp(params[span, here])
                    rates[span, here] = rate
                    mid[span, here] = x + rate * flow
                else:
                    value = x + rates[span, here] * flow
                    result[span, here] = value
                    top = value.astype(jnp.bfloat16)
                    rest = value - top.astype(jnp.float32)
                    middle = rest.astype(jnp.bfloat16)
                    last = (rest - middle.astype(jnp.float32)).astype(jnp.bfloat16)
                    split[span, here] = top
                    split[pl.ds(start + members, GROUP), here] = middle
                    split[pl.ds(start + 2 * members, GROUP), here] = last

    for copy in params_loads + state_loads:
        copy.wait()
    second = []
    for c in range(HALO_PARTS):
        for copy in first[c]:
            copy.wait()
        advance(state, 0, c)
        second.append(halo(mid, 1, c))
        if c == 1:
            send_params(9)
    for c in range(HALO_PARTS):
        for copy in second[c]:
            copy.wait()
        advance(mid, 1, c)

    state_stores = rowwise(result, state_out, store_sem, True)
    picked[...] = jnp.zeros_like(picked)
    depth = 1024

    @pl.loop(0, cells // depth)
    def _(b):
        span = pl.ds(pl.multiple_of(b * depth, depth), depth)
        picked[...] += jnp.dot(split[:, span], onehot[span, :], preferred_element_type=jnp.float32)

    own[...] = (picked[:members] + picked[members : 2 * members]) + picked[2 * members :]
    field = send(own, theirs, field_send, field_recv, twin)
    send_params(PARAM_PARTS)
    field.wait()

    everyone = 2 * members
    root = math.sqrt(everyone - 1)
    mean = (jnp.sum(own[...], axis=0, keepdims=True) + jnp.sum(theirs[...], axis=0, keepdims=True)) / everyone
    inverse = 1.0 / spread[...]
    scale = inverse / root
    stacked[:members] = (own[...] - mean) * scale
    stacked[members:everyone] = (theirs[...] - mean) * scale
    stacked[everyone:] = (measured[...] - own[...]) * inverse + jitter[...]
    contract = (((1,), (1,)), ((), ()))
    for h in range(2):
        part[h * members : (h + 1) * members] = lax.dot_general(
            stacked[h * members : (h + 1) * members], stacked[...], contract,
            precision=HIGHEST, preferred_element_type=jnp.float32,
        )

    start = 0
    size = everyone
    used = 0
    for t in range(low):
        size //= 2
        keep = pl.multiple_of(start + bits[t] * size, size)
        give = pl.multiple_of(start + (1 - bits[t]) * size, size)
        copy = send(part.at[pl.ds(give, size)], landed.at[pl.ds(used, size)],
                    sum_send.at[t], sum_recv.at[t], {"space": pairs[t]})
        copy.wait()
        part[pl.ds(keep, size)] = part[pl.ds(keep, size)] + landed[pl.ds(used, size)]
        used += size
        start = keep
    mine = pl.ds(start, size)
    for t in range(low, low + high):
        copy = send(part.at[mine], landed_high.at[t - low],
                    sum_send.at[t], sum_recv.at[t], {"space": pairs[t]})
        copy.wait()
        part[mine] = part[mine] + landed_high[t - low]
    total[mine] = part[mine]
    for t in reversed(range(low)):
        span = pl.ds(pl.multiple_of(start, size), size)
        slot = low + high + t
        copy = send(total.at[span], total.at[span],
                    sum_send.at[slot], sum_recv.at[slot], {"space": pairs[t]})
        copy.wait()
        start = start - bits[t] * size
        size *= 2
    sums_out[...] = total[...]
    for copy in params_copies + state_stores:
        copy.wait()


def solve_kernel(sums, params_hbm, theirs_hbm, out_hbm, work, params, params_theirs, out, sem):
    rows, columns = params_hbm.shape[1:]
    loads = []
    for whole, flat, i in ((params_hbm, params, 0), (theirs_hbm, params_theirs, 1)):
        for r in range(rows):
            loads.append(pltpu.make_async_copy(
                whole.at[:, r, :], flat.at[:, pl.ds(r * columns, columns)], sem.at[i, r]))
            loads[-1].start()
    everyone = sums.shape[0]
    members = everyone // 2
    width = sums.shape[1]
    r = lax.broadcasted_iota(jnp.int32, (everyone, width), 0)
    c = lax.broadcasted_iota(jnp.int32, (everyone, width), 1)
    work[...] = sums[...] + jnp.where(r == c, 1.0, 0.0)
    size = 32
    row = lax.broadcasted_iota(jnp.int32, (size, 2 * size), 0)
    lane = lax.broadcasted_iota(jnp.int32, (size, 2 * size), 1)
    unit = lax.broadcasted_iota(jnp.int32, (size, size), 0) == lax.broadcasted_iota(jnp.int32, (size, size), 1)
    for b in range(everyone // size):
        at = b * size
        pivot = work[at : at + size, at : at + size]
        aug = jnp.concatenate([pivot, jnp.where(unit, 1.0, 0.0)], axis=1)
        for k in range(size):
            line = aug[k : k + 1, :] / aug[k : k + 1, k : k + 1]
            aug = jnp.where(row == k, line, aug - aug[:, k : k + 1] * line)
        inverse = aug[:, size:]
        begin = (at + size) // 128 * 128
        lines = jnp.dot(inverse, work[at : at + size, begin:], precision=HIGHEST, preferred_element_type=jnp.float32)
        change = jnp.dot(work[:, at : at + size], lines, precision=HIGHEST, preferred_element_type=jnp.float32)
        work[:, begin:] = work[:, begin:] - change
        work[at : at + size, begin:] = lines
    mixing = work[:, everyone:] / math.sqrt(everyone - 1)
    weights = mixing.T
    tile = 512
    for copy in loads:
        copy.wait()
    stores = []
    for r in range(rows):
        @pl.loop(0, columns // tile)
        def _(b):
            span = pl.ds(pl.multiple_of(r * columns + b * tile, tile), tile)
            out[:, span] = params[:, span] + (
                jnp.dot(weights[:, :members], params[:, span], precision=HIGHEST, preferred_element_type=jnp.float32)
                + jnp.dot(weights[:, members:], params_theirs[:, span], precision=HIGHEST, preferred_element_type=jnp.float32)
            )
        stores.append(pltpu.make_async_copy(
            out.at[:, pl.ds(r * columns, columns)], out_hbm.at[:, r, :], sem.at[2, r]))
        stores[-1].start()
    for copy in stores:
        copy.wait()


def body(n, params, state, regime, regime_coefs, index, measured, spread, jitter):
    members, rows, columns = params.shape
    cells = rows * columns
    observations = index.shape[0]
    everyone = 2 * members
    levels = n.bit_length() - 1
    low = min(levels, 4)
    high = levels - low
    f32 = jnp.float32
    anywhere = pl.BlockSpec(memory_space=pl.ANY)
    flat = pltpu.VMEM((members, cells), f32)
    vmem = pl.BlockSpec(memory_space=pltpu.VMEM)
    smem = pl.BlockSpec(memory_space=pltpu.SMEM)
    width = everyone + members
    last = everyone >> low
    sems = pltpu.SemaphoreType.DMA
    state_out, theirs, sums = pl.pallas_call(
        functools.partial(forward_kernel, n, low, high),
        out_shape=[
            jax.ShapeDtypeStruct(state.shape, f32),
            jax.ShapeDtypeStruct(params.shape, f32),
            jax.ShapeDtypeStruct((everyone, width), f32),
        ],
        in_specs=[anywhere, anywhere, vmem, smem, vmem, vmem, vmem, vmem],
        out_specs=[anywhere, anywhere, vmem],
        scratch_shapes=[
            flat,
            flat,
            flat,
            flat,
            flat,
            pltpu.VMEM((4, rows, columns), f32),
            pltpu.VMEM((2, members, columns), f32),
            pltpu.VMEM((2, members, columns), f32),
            pltpu.VMEM((cells, observations), jnp.bfloat16),
            pltpu.VMEM((3 * members, cells), jnp.bfloat16),
            pltpu.VMEM((3 * members, observations), f32),
            pltpu.VMEM((members, observations), f32),
            pltpu.VMEM((members, observations), f32),
            pltpu.VMEM((3 * members, observations), f32),
            pltpu.VMEM((everyone, width), f32),
            pltpu.VMEM((everyone, width), f32),
            pltpu.VMEM((max(high, 1), last, width), f32),
            pltpu.VMEM((everyone, width), f32),
            sems((2, 2, HALO_PARTS)),
            sems((2, 2, HALO_PARTS)),
            sems((PARAM_PARTS,)),
            sems((PARAM_PARTS,)),
            sems,
            sems,
            sems((2 * low + high,)),
            sems((2 * low + high,)),
            sems((2, rows)),
            sems((rows,)),
        ],
        compiler_params=pltpu.CompilerParams(
            collective_id=0, has_side_effects=True, vmem_limit_bytes=48 << 20
        ),
    )(params, state, regime, regime_coefs, index[None], measured[None], spread[None], jitter)
    revised = pl.pallas_call(
        solve_kernel,
        out_shape=jax.ShapeDtypeStruct(params.shape, f32),
        in_specs=[vmem, anywhere, anywhere],
        out_specs=anywhere,
        scratch_shapes=[pltpu.VMEM((everyone, width), f32), flat, flat, flat, sems((3, rows))],
        compiler_params=pltpu.CompilerParams(vmem_limit_bytes=32 << 20),
    )(sums, params, theirs)
    return (revised, state_out)


def solution(mesh):
    in_specs = (
        P("member", "space", None),
        P("member", "space", None),
        P("space", None),
        P(),
        P("space"),
        P("space"),
        P("space"),
        P("member", "space"),
    )
    out_specs = (P("member", "space", None), P("member", "space", None))
    return jax.shard_map(
        functools.partial(body, mesh.shape["space"]),
        mesh=mesh, in_specs=in_specs, out_specs=out_specs, check_vma=False,
    )
```

```python
import functools
import math

import jax
import jax.numpy as jnp
from jax import lax
from jax.experimental import pallas as pl
from jax.experimental.pallas import tpu as pltpu
from jax.sharding import PartitionSpec as P

time_step = 0.06
MESH = pl.DeviceIdType.MESH
HIGHEST = lax.Precision.HIGHEST
HALO_PARTS = 4
PARAM_PARTS = 16
GROUP = 16


def forward_kernel(
    n, low, high, params_hbm, state_hbm, regime, regime_coefs, index, measured, spread, jitter,
    state_out, theirs_out, sums_out,
    params, state, result, mid, rates, coef, from_up, from_down, onehot, split, picked, own, theirs,
    stacked, part, landed, landed_high, total,
    halo_send, halo_recv, params_send, params_recv, field_send, field_recv, sum_send, sum_recv, load_sem, store_sem,
):
    members, cells = params.shape
    rows = regime.shape[0]
    columns = cells // rows
    me = lax.axis_index("space")
    up = lax.rem(me + n - 1, n)
    down = lax.rem(me + 1, n)
    twin = {"member": 1 - lax.axis_index("member")}
    bits = [lax.rem(lax.div(me, 1 << t), 2) for t in range(low + high)]
    pairs = [me + (1 - 2 * bits[t]) * (1 << t) for t in range(low + high)]

    def rowwise(flat, whole, sem, outward):
        copies = []
        for r in range(rows):
            pair = (flat.at[:, pl.ds(r * columns, columns)], whole.at[:, r, :])
            src, dst = pair if outward else pair[::-1]
            copies.append(pltpu.make_async_copy(src, dst, sem.at[r]))
            copies[-1].start()
        return copies

    params_loads = rowwise(params, params_hbm, load_sem.at[0], False)
    state_loads = rowwise(state, state_hbm, load_sem.at[1], False)

    barrier = pltpu.get_barrier_semaphore()
    greeted = [twin, {"space": up}, {"space": down}] + [{"space": q} for q in pairs]
    for device in greeted:
        pl.semaphore_signal(barrier, inc=1, device_id=device, device_id_type=MESH)
    pl.semaphore_wait(barrier, len(greeted))

    def send(src, dst, ssem, rsem, device):
        copy = pltpu.make_async_remote_copy(
            src_ref=src, dst_ref=dst, send_sem=ssem, recv_sem=rsem,
            device_id=device, device_id_type=MESH,
        )
        copy.start()
        return copy

    block = members // HALO_PARTS

    def halo(src, phase, c):
        span = pl.ds(c * block, block)
        if phase == 0:
            bottom, top = src.at[span, rows - 1, :], src.at[span, 0, :]
        else:
            bottom, top = src.at[span, pl.ds(cells - columns, columns)], src.at[span, pl.ds(0, columns)]
        return [
            send(bottom, from_up.at[phase, span],
                 halo_send.at[phase, 0, c], halo_recv.at[phase, 0, c], {"space": down}),
            send(top, from_down.at[phase, span],
                 halo_send.at[phase, 1, c], halo_recv.at[phase, 1, c], {"space": up}),
        ]

    params_rows = members // PARAM_PARTS
    params_copies = []

    def send_params(stop):
        for c in range(len(params_copies), stop):
            span = pl.ds(c * params_rows, params_rows)
            params_copies.append(send(params_hbm.at[span], theirs_out.at[span],
                                      params_send.at[c], params_recv.at[c], twin))

    first = [halo(state_hbm, 0, c) for c in range(HALO_PARTS)]
    send_params(6)

    for d in range(4):
        value = jnp.zeros(regime.shape, jnp.float32)
        for k in range(regime_coefs.shape[0]):
            value = jnp.where(regime[...] == k, regime_coefs[k, d], value)
        coef[d] = value

    observations = index.shape[1]
    local = index[...] - me * cells
    height = 256

    @pl.loop(0, cells // height)
    def _(b):
        start = pl.multiple_of(b * height, height)
        cell = lax.broadcasted_iota(jnp.int32, (height, observations), 0) + start
        onehot[pl.ds(start, height), :] = jnp.where(cell == local, 1.0, 0.0).astype(jnp.bfloat16)

    column = lax.broadcasted_iota(jnp.int32, (GROUP, columns), 1)

    def advance(src, phase, c):
        @pl.loop(0, block // GROUP)
        def _(g):
            start = pl.multiple_of(c * block + g * GROUP, GROUP)
            span = pl.ds(start, GROUP)
            for r in range(rows):
                here = pl.ds(r * columns, columns)
                x = src[span, here]
                if r > 0:
                    above = src[span, pl.ds((r - 1) * columns, columns)]
                else:
                    above = jnp.where(me > 0, from_up[phase, span, :], 0.0)
                if r < rows - 1:
                    below = src[span, pl.ds((r + 1) * columns, columns)]
                else:
                    below = jnp.where(me < n - 1, from_down[phase, span, :], 0.0)
                left = jnp.where(column == 0, 0.0, pltpu.roll(x, 1, 1))
                right = jnp.where(column == columns - 1, 0.0, pltpu.roll(x, columns - 1, 1))
                row = pl.ds(r, 1)
                flow = coef[0, row, :] * (above - x) + coef[1, row, :] * (below - x)
                flow = flow + coef[2, row, :] * (left - x) + coef[3, row, :] * (right - x)
                if phase == 0:
                    rate = time_step * jnp.exp(params[span, here])
                    rates[span, here] = rate
                    mid[span, here] = x + rate * flow
                else:
                    value = x + rates[span, here] * flow
                    result[span, here] = value
                    top = value.astype(jnp.bfloat16)
                    rest = value - top.astype(jnp.float32)
                    middle = rest.astype(jnp.bfloat16)
                    last = (rest - middle.astype(jnp.float32)).astype(jnp.bfloat16)
                    split[span, here] = top
                    split[pl.ds(start + members, GROUP), here] = middle
                    split[pl.ds(start + 2 * members, GROUP), here] = last

    for copy in params_loads + state_loads:
        copy.wait()
    second = []
    for c in range(HALO_PARTS):
        for copy in first[c]:
            copy.wait()
        advance(state, 0, c)
        second.append(halo(mid, 1, c))
        if c == 1:
            send_params(9)
    for c in range(HALO_PARTS):
        for copy in second[c]:
            copy.wait()
        advance(mid, 1, c)

    state_stores = rowwise(result, state_out, store_sem, True)
    picked[...] = jnp.zeros_like(picked)
    depth = 1024

    @pl.loop(0, cells // depth)
    def _(b):
        span = pl.ds(pl.multiple_of(b * depth, depth), depth)
        picked[...] += jnp.dot(split[:, span], onehot[span, :], preferred_element_type=jnp.float32)

    own[...] = (picked[:members] + picked[members : 2 * members]) + picked[2 * members :]
    field = send(own, theirs, field_send, field_recv, twin)
    send_params(PARAM_PARTS)
    field.wait()

    everyone = 2 * members
    root = math.sqrt(everyone - 1)
    mean = (jnp.sum(own[...], axis=0, keepdims=True) + jnp.sum(theirs[...], axis=0, keepdims=True)) / everyone
    inverse = 1.0 / spread[...]
    scale = inverse / root
    stacked[:members] = (own[...] - mean) * scale
    stacked[members:everyone] = (theirs[...] - mean) * scale
    stacked[everyone:] = (measured[...] - own[...]) * inverse + jitter[...]
    contract = (((1,), (1,)), ((), ()))
    for h in range(2):
        part[h * members : (h + 1) * members] = lax.dot_general(
            stacked[h * members : (h + 1) * members], stacked[...], contract,
            precision=HIGHEST, preferred_element_type=jnp.float32,
        )

    start = 0
    size = everyone
    used = 0
    for t in range(low):
        size //= 2
        keep = pl.multiple_of(start + bits[t] * size, size)
        give = pl.multiple_of(start + (1 - bits[t]) * size, size)
        copy = send(part.at[pl.ds(give, size)], landed.at[pl.ds(used, size)],
                    sum_send.at[t], sum_recv.at[t], {"space": pairs[t]})
        copy.wait()
        part[pl.ds(keep, size)] = part[pl.ds(keep, size)] + landed[pl.ds(used, size)]
        used += size
        start = keep
    mine = pl.ds(start, size)
    for t in range(low, low + high):
        copy = send(part.at[mine], landed_high.at[t - low],
                    sum_send.at[t], sum_recv.at[t], {"space": pairs[t]})
        copy.wait()
        part[mine] = part[mine] + landed_high[t - low]
    total[mine] = part[mine]
    for t in reversed(range(low)):
        span = pl.ds(pl.multiple_of(start, size), size)
        slot = low + high + t
        copy = send(total.at[span], total.at[span],
                    sum_send.at[slot], sum_recv.at[slot], {"space": pairs[t]})
        copy.wait()
        start = start - bits[t] * size
        size *= 2
    sums_out[...] = total[...]
    for copy in params_copies + state_stores:
        copy.wait()


def solve_kernel(sums, params_hbm, theirs_hbm, out_hbm, work, params, params_theirs, out, sem):
    rows, columns = params_hbm.shape[1:]
    loads = []
    for whole, flat, i in ((params_hbm, params, 0), (theirs_hbm, params_theirs, 1)):
        for r in range(rows):
            loads.append(pltpu.make_async_copy(
                whole.at[:, r, :], flat.at[:, pl.ds(r * columns, columns)], sem.at[i, r]))
            loads[-1].start()
    everyone = sums.shape[0]
    members = everyone // 2
    width = sums.shape[1]
    r = lax.broadcasted_iota(jnp.int32, (everyone, width), 0)
    c = lax.broadcasted_iota(jnp.int32, (everyone, width), 1)
    work[...] = sums[...] + jnp.where(r == c, 1.0, 0.0)
    size = 64
    row = lax.broadcasted_iota(jnp.int32, (size, 2 * size), 0)
    lane = lax.broadcasted_iota(jnp.int32, (size, 2 * size), 1)
    unit = lax.broadcasted_iota(jnp.int32, (size, size), 0) == lax.broadcasted_iota(jnp.int32, (size, size), 1)
    for b in range(everyone // size):
        at = b * size
        pivot = work[at : at + size, at : at + size]
        aug = jnp.concatenate([pivot, jnp.where(unit, 1.0, 0.0)], axis=1)
        for k in range(0, size, 2):
            col0 = jnp.broadcast_to(aug[:, k : k + 1], aug.shape)
            col1 = jnp.broadcast_to(aug[:, k + 1 : k + 2], aug.shape)
            p00, p01 = col0[k : k + 1, :], col1[k : k + 1, :]
            p11 = col1[k + 1 : k + 2, :]
            scale = 1.0 / (p00 * p11 - p01 * p01)
            row0, row1 = aug[k : k + 1, :], aug[k + 1 : k + 2, :]
            line0 = (p11 * row0 - p01 * row1) * scale
            line1 = (p00 * row1 - p01 * row0) * scale
            aug = aug - col0 * line0 - col1 * line1
            aug = jnp.where(row == k, line0, jnp.where(row == k + 1, line1, aug))
        inverse = aug[:, size:]
        begin = (at + size) // 128 * 128
        lines = jnp.dot(inverse, work[at : at + size, begin:], precision=HIGHEST, preferred_element_type=jnp.float32)
        change = jnp.dot(work[:, at : at + size], lines, precision=HIGHEST, preferred_element_type=jnp.float32)
        work[:, begin:] = work[:, begin:] - change
        work[at : at + size, begin:] = lines
    mixing = work[:, everyone:] / math.sqrt(everyone - 1)
    weights = mixing.T
    heavy = weights.astype(jnp.bfloat16)
    light = (weights - heavy.astype(jnp.float32)).astype(jnp.bfloat16)
    tile = 512
    for copy in loads:
        copy.wait()
    stores = []
    for r in range(rows):
        @pl.loop(0, columns // tile)
        def _(b):
            span = pl.ds(pl.multiple_of(r * columns + b * tile, tile), tile)
            piece = jnp.concatenate([params[:, span], params_theirs[:, span]], axis=0)
            top = piece.astype(jnp.bfloat16)
            rest = (piece - top.astype(jnp.float32)).astype(jnp.bfloat16)
            update = jnp.dot(heavy, top, preferred_element_type=jnp.float32)
            update += jnp.dot(heavy, rest, preferred_element_type=jnp.float32)
            update += jnp.dot(light, top, preferred_element_type=jnp.float32)
            out[:, span] = params[:, span] + update
        stores.append(pltpu.make_async_copy(
            out.at[:, pl.ds(r * columns, columns)], out_hbm.at[:, r, :], sem.at[2, r]))
        stores[-1].start()
    for copy in stores:
        copy.wait()


def body(n, params, state, regime, regime_coefs, index, measured, spread, jitter):
    members, rows, columns = params.shape
    cells = rows * columns
    observations = index.shape[0]
    everyone = 2 * members
    levels = n.bit_length() - 1
    low = min(levels, 4)
    high = levels - low
    f32 = jnp.float32
    anywhere = pl.BlockSpec(memory_space=pl.ANY)
    flat = pltpu.VMEM((members, cells), f32)
    vmem = pl.BlockSpec(memory_space=pltpu.VMEM)
    smem = pl.BlockSpec(memory_space=pltpu.SMEM)
    width = everyone + members
    last = everyone >> low
    sems = pltpu.SemaphoreType.DMA
    state_out, theirs, sums = pl.pallas_call(
        functools.partial(forward_kernel, n, low, high),
        out_shape=[
            jax.ShapeDtypeStruct(state.shape, f32),
            jax.ShapeDtypeStruct(params.shape, f32),
            jax.ShapeDtypeStruct((everyone, width), f32),
        ],
        in_specs=[anywhere, anywhere, vmem, smem, vmem, vmem, vmem, vmem],
        out_specs=[anywhere, anywhere, vmem],
        scratch_shapes=[
            flat,
            flat,
            flat,
            flat,
            flat,
            pltpu.VMEM((4, rows, columns), f32),
            pltpu.VMEM((2, members, columns), f32),
            pltpu.VMEM((2, members, columns), f32),
            pltpu.VMEM((cells, observations), jnp.bfloat16),
            pltpu.VMEM((3 * members, cells), jnp.bfloat16),
            pltpu.VMEM((3 * members, observations), f32),
            pltpu.VMEM((members, observations), f32),
            pltpu.VMEM((members, observations), f32),
            pltpu.VMEM((3 * members, observations), f32),
            pltpu.VMEM((everyone, width), f32),
            pltpu.VMEM((everyone, width), f32),
            pltpu.VMEM((max(high, 1), last, width), f32),
            pltpu.VMEM((everyone, width), f32),
            sems((2, 2, HALO_PARTS)),
            sems((2, 2, HALO_PARTS)),
            sems((PARAM_PARTS,)),
            sems((PARAM_PARTS,)),
            sems,
            sems,
            sems((2 * low + high,)),
            sems((2 * low + high,)),
            sems((2, rows)),
            sems((rows,)),
        ],
        compiler_params=pltpu.CompilerParams(
            collective_id=0, has_side_effects=True, vmem_limit_bytes=48 << 20
        ),
    )(params, state, regime, regime_coefs, index[None], measured[None], spread[None], jitter)
    revised = pl.pallas_call(
        solve_kernel,
        out_shape=jax.ShapeDtypeStruct(params.shape, f32),
        in_specs=[vmem, anywhere, anywhere],
        out_specs=anywhere,
        scratch_shapes=[pltpu.VMEM((everyone, width), f32), flat, flat, flat, sems((3, rows))],
        compiler_params=pltpu.CompilerParams(vmem_limit_bytes=32 << 20),
    )(sums, params, theirs)
    return (revised, state_out)


def solution(mesh):
    in_specs = (
        P("member", "space", None),
        P("member", "space", None),
        P("space", None),
        P(),
        P("space"),
        P("space"),
        P("space"),
        P("member", "space"),
    )
    out_specs = (P("member", "space", None), P("member", "space", None))
    return jax.shard_map(
        functools.partial(body, mesh.shape["space"]),
        mesh=mesh, in_specs=in_specs, out_specs=out_specs, check_vma=False,
    )
```

```python
import functools
import math

import jax
import jax.numpy as jnp
from jax import lax
from jax.experimental import pallas as pl
from jax.experimental.pallas import tpu as pltpu
from jax.sharding import PartitionSpec as P

time_step = 0.06
MESH = pl.DeviceIdType.MESH
HIGHEST = lax.Precision.HIGHEST
HALO_PARTS = 4
PARAM_PARTS = 16
GROUP = 16


def forward_kernel(
    n, low, high, params_hbm, state_hbm, regime_hbm, regime_coefs, index_hbm, measured_hbm, spread_hbm, jitter_hbm,
    state_out, theirs_out, sums_out,
    params, state, result, mid, rates, coef, from_up, from_down, onehot, split, picked, own, theirs,
    stacked, part, landed, landed_high, total,
    halo_send, halo_recv, params_send, params_recv, field_send, field_recv, sum_send, sum_recv, load_sem, store_sem,
    regime, index, measured, spread, jitter, small_sem,
):
    members, cells = params.shape
    rows = regime.shape[0]
    columns = cells // rows
    me = lax.axis_index("space")
    up = lax.rem(me + n - 1, n)
    down = lax.rem(me + 1, n)
    twin = {"member": 1 - lax.axis_index("member")}
    bits = [lax.rem(lax.div(me, 1 << t), 2) for t in range(low + high)]
    pairs = [me + (1 - 2 * bits[t]) * (1 << t) for t in range(low + high)]

    def rowwise(flat, whole, sem, outward):
        copies = []
        for r in range(rows):
            pair = (flat.at[:, pl.ds(r * columns, columns)], whole.at[:, r, :])
            src, dst = pair if outward else pair[::-1]
            copies.append(pltpu.make_async_copy(src, dst, sem.at[r]))
            copies[-1].start()
        return copies

    small_loads = []
    for i, (src, dst) in enumerate([
        (regime_hbm, regime), (index_hbm, index), (measured_hbm, measured), (spread_hbm, spread), (jitter_hbm, jitter),
    ]):
        small_loads.append(pltpu.make_async_copy(src, dst, small_sem.at[i]))
        small_loads[-1].start()
    params_loads = rowwise(params, params_hbm, load_sem.at[0], False)
    state_loads = rowwise(state, state_hbm, load_sem.at[1], False)

    barrier = pltpu.get_barrier_semaphore()
    greeted = [twin, {"space": up}, {"space": down}] + [{"space": q} for q in pairs]
    for device in greeted:
        pl.semaphore_signal(barrier, inc=1, device_id=device, device_id_type=MESH)
    pl.semaphore_wait(barrier, len(greeted))

    def send(src, dst, ssem, rsem, device):
        copy = pltpu.make_async_remote_copy(
            src_ref=src, dst_ref=dst, send_sem=ssem, recv_sem=rsem,
            device_id=device, device_id_type=MESH,
        )
        copy.start()
        return copy

    block = members // HALO_PARTS

    def halo(src, phase, c):
        span = pl.ds(c * block, block)
        if phase == 0:
            bottom, top = src.at[span, rows - 1, :], src.at[span, 0, :]
        else:
            bottom, top = src.at[span, pl.ds(cells - columns, columns)], src.at[span, pl.ds(0, columns)]
        return [
            send(bottom, from_up.at[phase, span],
                 halo_send.at[phase, 0, c], halo_recv.at[phase, 0, c], {"space": down}),
            send(top, from_down.at[phase, span],
                 halo_send.at[phase, 1, c], halo_recv.at[phase, 1, c], {"space": up}),
        ]

    params_rows = members // PARAM_PARTS
    params_copies = []

    def send_params(stop):
        for c in range(len(params_copies), stop):
            span = pl.ds(c * params_rows, params_rows)
            params_copies.append(send(params_hbm.at[span], theirs_out.at[span],
                                      params_send.at[c], params_recv.at[c], twin))

    first = [halo(state_hbm, 0, c) for c in range(HALO_PARTS)]
    send_params(6)

    for copy in small_loads:
        copy.wait()
    for d in range(4):
        value = jnp.zeros(regime.shape, jnp.float32)
        for k in range(regime_coefs.shape[0]):
            value = jnp.where(regime[...] == k, regime_coefs[k, d], value)
        coef[d] = value

    observations = index.shape[1]
    local = index[...] - me * cells
    height = 256

    @pl.loop(0, cells // height)
    def _(b):
        start = pl.multiple_of(b * height, height)
        cell = lax.broadcasted_iota(jnp.int32, (height, observations), 0) + start
        onehot[pl.ds(start, height), :] = jnp.where(cell == local, 1.0, 0.0).astype(jnp.bfloat16)

    column = lax.broadcasted_iota(jnp.int32, (GROUP, columns), 1)

    def advance(src, phase, c):
        @pl.loop(0, block // GROUP)
        def _(g):
            start = pl.multiple_of(c * block + g * GROUP, GROUP)
            span = pl.ds(start, GROUP)
            for r in range(rows):
                here = pl.ds(r * columns, columns)
                x = src[span, here]
                if r > 0:
                    above = src[span, pl.ds((r - 1) * columns, columns)]
                else:
                    above = jnp.where(me > 0, from_up[phase, span, :], 0.0)
                if r < rows - 1:
                    below = src[span, pl.ds((r + 1) * columns, columns)]
                else:
                    below = jnp.where(me < n - 1, from_down[phase, span, :], 0.0)
                left = jnp.where(column == 0, 0.0, pltpu.roll(x, 1, 1))
                right = jnp.where(column == columns - 1, 0.0, pltpu.roll(x, columns - 1, 1))
                row = pl.ds(r, 1)
                flow = coef[0, row, :] * (above - x) + coef[1, row, :] * (below - x)
                flow = flow + coef[2, row, :] * (left - x) + coef[3, row, :] * (right - x)
                if phase == 0:
                    rate = time_step * jnp.exp(params[span, here])
                    rates[span, here] = rate
                    mid[span, here] = x + rate * flow
                else:
                    value = x + rates[span, here] * flow
                    result[span, here] = value
                    top = value.astype(jnp.bfloat16)
                    rest = value - top.astype(jnp.float32)
                    middle = rest.astype(jnp.bfloat16)
                    last = (rest - middle.astype(jnp.float32)).astype(jnp.bfloat16)
                    split[span, here] = top
                    split[pl.ds(start + members, GROUP), here] = middle
                    split[pl.ds(start + 2 * members, GROUP), here] = last

    for copy in params_loads + state_loads:
        copy.wait()
    second = []
    for c in range(HALO_PARTS):
        for copy in first[c]:
            copy.wait()
        advance(state, 0, c)
        second.append(halo(mid, 1, c))
        if c == 1:
            send_params(9)
    for c in range(HALO_PARTS):
        for copy in second[c]:
            copy.wait()
        advance(mid, 1, c)

    state_stores = rowwise(result, state_out, store_sem, True)
    picked[...] = jnp.zeros_like(picked)
    depth = 1024

    @pl.loop(0, cells // depth)
    def _(b):
        span = pl.ds(pl.multiple_of(b * depth, depth), depth)
        picked[...] += jnp.dot(split[:, span], onehot[span, :], preferred_element_type=jnp.float32)

    own[...] = (picked[:members] + picked[members : 2 * members]) + picked[2 * members :]
    field = send(own, theirs, field_send, field_recv, twin)
    send_params(PARAM_PARTS)
    field.wait()

    everyone = 2 * members
    root = math.sqrt(everyone - 1)
    mean = (jnp.sum(own[...], axis=0, keepdims=True) + jnp.sum(theirs[...], axis=0, keepdims=True)) / everyone
    inverse = 1.0 / spread[...]
    scale = inverse / root
    stacked[:members] = (own[...] - mean) * scale
    stacked[members:everyone] = (theirs[...] - mean) * scale
    stacked[everyone:] = (measured[...] - own[...]) * inverse + jitter[...]
    contract = (((1,), (1,)), ((), ()))
    for h in range(2):
        part[h * members : (h + 1) * members] = lax.dot_general(
            stacked[h * members : (h + 1) * members], stacked[...], contract,
            precision=HIGHEST, preferred_element_type=jnp.float32,
        )

    start = 0
    size = everyone
    used = 0
    for t in range(low):
        size //= 2
        keep = pl.multiple_of(start + bits[t] * size, size)
        give = pl.multiple_of(start + (1 - bits[t]) * size, size)
        copy = send(part.at[pl.ds(give, size)], landed.at[pl.ds(used, size)],
                    sum_send.at[t], sum_recv.at[t], {"space": pairs[t]})
        copy.wait()
        part[pl.ds(keep, size)] = part[pl.ds(keep, size)] + landed[pl.ds(used, size)]
        used += size
        start = keep
    mine = pl.ds(start, size)
    for t in range(low, low + high):
        copy = send(part.at[mine], landed_high.at[t - low],
                    sum_send.at[t], sum_recv.at[t], {"space": pairs[t]})
        copy.wait()
        part[mine] = part[mine] + landed_high[t - low]
    total[mine] = part[mine]
    for t in reversed(range(low)):
        span = pl.ds(pl.multiple_of(start, size), size)
        slot = low + high + t
        copy = send(total.at[span], total.at[span],
                    sum_send.at[slot], sum_recv.at[slot], {"space": pairs[t]})
        copy.wait()
        start = start - bits[t] * size
        size *= 2
    sums_out[...] = total[...]
    for copy in params_copies + state_stores:
        copy.wait()


def solve_kernel(sums, params_hbm, theirs_hbm, out_hbm, work, params, params_theirs, out, sem):
    rows, columns = params_hbm.shape[1:]
    loads = []
    for whole, flat, i in ((params_hbm, params, 0), (theirs_hbm, params_theirs, 1)):
        for r in range(rows):
            loads.append(pltpu.make_async_copy(
                whole.at[:, r, :], flat.at[:, pl.ds(r * columns, columns)], sem.at[i, r]))
            loads[-1].start()
    everyone = sums.shape[0]
    members = everyone // 2
    width = sums.shape[1]
    r = lax.broadcasted_iota(jnp.int32, (everyone, width), 0)
    c = lax.broadcasted_iota(jnp.int32, (everyone, width), 1)
    work[...] = sums[...] + jnp.where(r == c, 1.0, 0.0)
    size = 64
    row = lax.broadcasted_iota(jnp.int32, (size, 2 * size), 0)
    lane = lax.broadcasted_iota(jnp.int32, (size, 2 * size), 1)
    unit = lax.broadcasted_iota(jnp.int32, (size, size), 0) == lax.broadcasted_iota(jnp.int32, (size, size), 1)
    for b in range(everyone // size):
        at = b * size
        pivot = work[at : at + size, at : at + size]
        aug = jnp.concatenate([pivot, jnp.where(unit, 1.0, 0.0)], axis=1)
        for k in range(0, size, 2):
            col0 = jnp.broadcast_to(aug[:, k : k + 1], aug.shape)
            col1 = jnp.broadcast_to(aug[:, k + 1 : k + 2], aug.shape)
            p00, p01 = col0[k : k + 1, :], col1[k : k + 1, :]
            p11 = col1[k + 1 : k + 2, :]
            scale = 1.0 / (p00 * p11 - p01 * p01)
            row0, row1 = aug[k : k + 1, :], aug[k + 1 : k + 2, :]
            line0 = (p11 * row0 - p01 * row1) * scale
            line1 = (p00 * row1 - p01 * row0) * scale
            aug = aug - col0 * line0 - col1 * line1
            aug = jnp.where(row == k, line0, jnp.where(row == k + 1, line1, aug))
        inverse = aug[:, size:]
        begin = (at + size) // 128 * 128
        lines = jnp.dot(inverse, work[at : at + size, begin:], precision=HIGHEST, preferred_element_type=jnp.float32)
        change = jnp.dot(work[:, at : at + size], lines, precision=HIGHEST, preferred_element_type=jnp.float32)
        work[:, begin:] = work[:, begin:] - change
        work[at : at + size, begin:] = lines
    mixing = work[:, everyone:] / math.sqrt(everyone - 1)
    weights = mixing.T
    heavy = weights.astype(jnp.bfloat16)
    light = (weights - heavy.astype(jnp.float32)).astype(jnp.bfloat16)
    tile = 512
    for copy in loads:
        copy.wait()
    stores = []
    for r in range(rows):
        @pl.loop(0, columns // tile)
        def _(b):
            span = pl.ds(pl.multiple_of(r * columns + b * tile, tile), tile)
            piece = jnp.concatenate([params[:, span], params_theirs[:, span]], axis=0)
            top = piece.astype(jnp.bfloat16)
            rest = (piece - top.astype(jnp.float32)).astype(jnp.bfloat16)
            update = jnp.dot(heavy, top, preferred_element_type=jnp.float32)
            update += jnp.dot(heavy, rest, preferred_element_type=jnp.float32)
            update += jnp.dot(light, top, preferred_element_type=jnp.float32)
            out[:, span] = params[:, span] + update
        stores.append(pltpu.make_async_copy(
            out.at[:, pl.ds(r * columns, columns)], out_hbm.at[:, r, :], sem.at[2, r]))
        stores[-1].start()
    for copy in stores:
        copy.wait()


def body(n, params, state, regime, regime_coefs, index, measured, spread, jitter):
    members, rows, columns = params.shape
    cells = rows * columns
    observations = index.shape[0]
    everyone = 2 * members
    levels = n.bit_length() - 1
    low = min(levels, 4)
    high = levels - low
    f32 = jnp.float32
    anywhere = pl.BlockSpec(memory_space=pl.ANY)
    hbm = pl.BlockSpec(memory_space=pltpu.HBM)
    flat = pltpu.VMEM((members, cells), f32)
    vmem = pl.BlockSpec(memory_space=pltpu.VMEM)
    smem = pl.BlockSpec(memory_space=pltpu.SMEM)
    width = everyone + members
    last = everyone >> low
    sems = pltpu.SemaphoreType.DMA
    state_out, theirs, sums = pl.pallas_call(
        functools.partial(forward_kernel, n, low, high),
        out_shape=[
            jax.ShapeDtypeStruct(state.shape, f32),
            jax.ShapeDtypeStruct(params.shape, f32),
            jax.ShapeDtypeStruct((everyone, width), f32),
        ],
        in_specs=[anywhere, anywhere, hbm, smem, hbm, hbm, hbm, hbm],
        out_specs=[anywhere, anywhere, vmem],
        scratch_shapes=[
            flat,
            flat,
            flat,
            flat,
            flat,
            pltpu.VMEM((4, rows, columns), f32),
            pltpu.VMEM((2, members, columns), f32),
            pltpu.VMEM((2, members, columns), f32),
            pltpu.VMEM((cells, observations), jnp.bfloat16),
            pltpu.VMEM((3 * members, cells), jnp.bfloat16),
            pltpu.VMEM((3 * members, observations), f32),
            pltpu.VMEM((members, observations), f32),
            pltpu.VMEM((members, observations), f32),
            pltpu.VMEM((3 * members, observations), f32),
            pltpu.VMEM((everyone, width), f32),
            pltpu.VMEM((everyone, width), f32),
            pltpu.VMEM((max(high, 1), last, width), f32),
            pltpu.VMEM((everyone, width), f32),
            sems((2, 2, HALO_PARTS)),
            sems((2, 2, HALO_PARTS)),
            sems((PARAM_PARTS,)),
            sems((PARAM_PARTS,)),
            sems,
            sems,
            sems((2 * low + high,)),
            sems((2 * low + high,)),
            sems((2, rows)),
            sems((rows,)),
            pltpu.VMEM(regime.shape, jnp.int32),
            pltpu.VMEM((1, observations), jnp.int32),
            pltpu.VMEM((1, observations), f32),
            pltpu.VMEM((1, observations), f32),
            pltpu.VMEM(jitter.shape, f32),
            sems((5,)),
        ],
        compiler_params=pltpu.CompilerParams(
            collective_id=0, has_side_effects=True, vmem_limit_bytes=62 << 20
        ),
    )(params, state, regime, regime_coefs, index[None], measured[None], spread[None], jitter)
    revised = pl.pallas_call(
        solve_kernel,
        out_shape=jax.ShapeDtypeStruct(params.shape, f32),
        in_specs=[vmem, anywhere, anywhere],
        out_specs=anywhere,
        scratch_shapes=[pltpu.VMEM((everyone, width), f32), flat, flat, flat, sems((3, rows))],
        compiler_params=pltpu.CompilerParams(vmem_limit_bytes=32 << 20),
    )(sums, params, theirs)
    return (revised, state_out)


def solution(mesh):
    in_specs = (
        P("member", "space", None),
        P("member", "space", None),
        P("space", None),
        P(),
        P("space"),
        P("space"),
        P("space"),
        P("member", "space"),
    )
    out_specs = (P("member", "space", None), P("member", "space", None))
    return jax.shard_map(
        functools.partial(body, mesh.shape["space"]),
        mesh=mesh, in_specs=in_specs, out_specs=out_specs, check_vma=False,
    )
```
